32 devices in a mesh: shard: 4 (over y, x), context: 4 (over z), tensor: 2 (over core).
Axes of the slice: x: 2, y: 2, z: 4, core: 2. Of those that a mesh axis runs over, the one named last changes fastest.
Arguments:
- hidden_in: bfloat16 [4, 1024, 1024], P('shard', 'context'), may hold values from -6 to 6
- norm_gain: float32 [1024], replicated, may hold values from 0.5 to 1.5
- mamba_in: bfloat16 [1024, 2, 1536], P('shard', None, 'tensor'), may hold values from -0.1875 to 0.1875
- mamba_bc: bfloat16 [1024, 256], P('shard'), may hold values from -0.1875 to 0.1875
- mamba_dt: bfloat16 [1024, 24], P('shard', 'tensor'), may hold values from -0.1875 to 0.1875
- dt_bias: float32 [24], P('tensor'), may hold values from -1 to 0.5
- decay_seed: int32 [24], P('tensor'), may hold values from 0 to 9, as said below
- conv_x: float32 [4, 1536], P(None, 'tensor'), may hold values from -3 to 3
- conv_bc: float32 [4, 256], replicated, may hold values from -3 to 3
- skip_d: float32 [24], P('tensor'), may hold values from 0.5 to 2
- ssm_gain: float32 [1536], P('tensor'), may hold values from 0.5 to 1.5
- mamba_out: bfloat16 [1536, 1024], P('tensor', 'shard'), may hold values from -0.15625 to 0.15625
- attn_q: bfloat16 [1024, 512], P('shard', 'tensor'), may hold values from -0.1875 to 0.1875
- attn_kv: bfloat16 [1024, 2, 128], P('shard', None, 'tensor'), may hold values from -0.1875 to 0.1875
- attn_out: bfloat16 [512, 1024], P('tensor', 'shard'), may hold values from -1 to 1
- mlp_gain: float32 [1024], replicated, may hold values from 0.5 to 1.5
- mlp_gate_up: bfloat16 [1024, 2, 2048], P('shard', None, 'tensor'), may hold values from -0.1875 to 0.1875
- mlp_down: bfloat16 [2048, 1024], P('tensor', 'shard'), may hold values from -0.125 to 0.125
- cotangent: bfloat16 [4, 1024, 1024], P('shard', 'context'), may hold values from -6 to 6
Outputs:
- block_out: bfloat16 [4, 1024, 1024], P('shard', 'context')
- grad_input: bfloat16 [4, 1024, 1024], P('shard', 'context')
- grad_norm_gain: float32 [1024], replicated
- grad_mamba_in: float32 [1024, 2, 1536], P(('shard', 'context'), None, 'tensor')
- grad_mamba_bc: float32 [1024, 256], P(('shard', 'context'))
- grad_mamba_dt: float32 [1024, 24], P(('shard', 'context'), 'tensor')
- grad_dt_bias: float32 [24], P('tensor')
- grad_conv_x: float32 [4, 1536], P(None, 'tensor')
- grad_conv_bc: float32 [4, 256], replicated
- grad_skip_d: float32 [24], P('tensor')
- grad_ssm_gain: float32 [1536], P('tensor')
- grad_mamba_out: float32 [1536, 1024], P('tensor', ('shard', 'context'))
- grad_attn_q: float32 [1024, 512], P(('shard', 'context'), 'tensor')
- grad_attn_kv: float32 [1024, 2, 128], P(('shard', 'context'), None, 'tensor')
- grad_attn_out: float32 [512, 1024], P('tensor', ('shard', 'context'))
- grad_mlp_gain: float32 [1024], replicated
- grad_mlp_gate_up: float32 [1024, 2, 2048], P(('shard', 'context'), None, 'tensor')
- grad_mlp_down: float32 [2048, 1024], P('tensor', ('shard', 'context'))
The draws below stay inside these ranges and needn't reach their ends.
Inputs may be any that keep to these rules, and one draw needn't show every extreme that they name: `decay_seed`: each head's decay seed is a whole number; with 10 or more heads every value from 0 to 9 occurs.
All inputs are finite; a program needn't handle non-finite values.
Results may differ from the reference program's by a relative error of at most 0.015.
The reference program's roundings to bfloat16 on the way count: a program that leaves them out, or rounds other values in their place, can miss the bound.
Values may be sent and summed in bfloat16 or wider, within the bound.
A program may use at most 128 MiB of HBM per device.

```python
import jax
import jax.numpy as jnp
from jax import lax

D = 1024
HQ = 8
KV = 2
HD = 64
HM = 24
STATE = 128
CONV = 4
FF = 2048
TOK_DEV = 256
SEQS = 4
LEN = 1024
DSSM = 1536


def draw_decay_seed(key, part):
    key = jax.random.fold_in(key, 7)
    order = jax.random.permutation(key, HM)
    return (order % 10).astype(jnp.int32)


def level_of(rng, extent, cuts, least, high):
    level = 1.0
    for dim, blocks in cuts:
        steps = jax.random.uniform(jax.random.fold_in(jax.random.fold_in(rng, 6), dim), (blocks,), jnp.float32, least / len(cuts), high / len(cuts))
        level = level * jnp.repeat(jnp.exp(steps), extent[dim] // blocks).reshape((-1,) + (1,) * (len(extent) - 1 - dim))
    return level


def noise(stream_key, shape, width, limit, split=(), kind=jnp.bfloat16):
    level = level_of(stream_key, shape, split, -0.22, 0.18) if split else 1.0
    drawn = jax.random.normal(stream_key, shape, jnp.float32) * width * level
    return jnp.minimum(jnp.maximum(drawn, -limit), limit).astype(kind)


def setup_inputs(seed: int = 0) -> dict:
    splits = jax.random.split(jax.random.key(seed), 20)
    return {
        "hidden_in": noise(splits[0], (SEQS, LEN, D), 1.0, 6.0, ((0, 4), (1, 4))),
        "norm_gain": jnp.clip(1.0 + 0.1 * jax.random.normal(splits[1], (D,), jnp.float32), 0.5, 1.5),
        "mamba_in": noise(splits[2], (D, 2, DSSM), D ** -0.5, 0.1875, ((0, 4), (2, 2))),
        "mamba_bc": noise(splits[3], (D, 2 * STATE), D ** -0.5, 0.1875, ((0, 4),)),
        "mamba_dt": noise(splits[4], (D, HM), D ** -0.5, 0.1875, ((0, 4), (1, 2))),
        "dt_bias": jnp.clip(-1.0 + 1.5 * jax.random.uniform(splits[5], (HM,), jnp.float32) ** level_of(splits[5], (HM,), ((0, 2),), -0.2, 0.2), -1.0, 0.5),
        "decay_seed": draw_decay_seed(jax.random.fold_in(splits[19], 71), 0),
        "conv_x": noise(splits[7], (CONV, DSSM), CONV ** -0.5, 3.0, ((1, 2),), jnp.float32),
        "conv_bc": noise(splits[8], (CONV, 2 * STATE), CONV ** -0.5, 3.0, (), jnp.float32),
        "skip_d": jnp.clip(0.5 + 1.5 * jax.random.uniform(splits[9], (HM,), jnp.float32) ** level_of(splits[9], (HM,), ((0, 2),), -0.2, 0.2), 0.5, 2.0),
        "ssm_gain": jnp.clip(1.0 + 0.1 * jax.random.normal(splits[10], (DSSM,), jnp.float32), 0.5, 1.5),
        "mamba_out": noise(splits[11], (DSSM, D), DSSM ** -0.5, 0.15625, ((0, 2), (1, 4))),
        "attn_q": noise(splits[12], (D, HQ * HD), D ** -0.5, 0.1875, ((0, 4), (1, 2))),
        "attn_kv": noise(splits[13], (D, 2, KV * HD), D ** -0.5, 0.1875, ((0, 4), (2, 2))),
        "attn_out": noise(splits[14], (HQ * HD, D), (HQ * HD // 16) ** -0.5, 1.0, ((0, 2), (1, 4))),
        "mlp_gain": jnp.clip(1.0 + 0.1 * jax.random.normal(splits[15], (D,), jnp.float32), 0.5, 1.5),
        "mlp_gate_up": noise(splits[16], (D, 2, FF), D ** -0.5, 0.1875, ((0, 4), (2, 2))),
        "mlp_down": noise(splits[17], (FF, D), FF ** -0.5, 0.125, ((0, 2), (1, 4))),
        "cotangent": noise(splits[18], (SEQS, LEN, D), 1.0, 6.0, ((0, 4), (1, 4))),
    }


epsilon = 1e-05
rope_base = 100000000000.0

@jax.custom_vjp
def low(v):
    return lax.optimization_barrier(v.astype(jnp.bfloat16)).astype(jnp.float32)

@jax.custom_vjp
def low_back(v):
    return v

def low_keep(v):
    return (low(v), None)

def low_pass(kept, grad):
    return (grad,)

def back_keep(v):
    return (v, None)

def back_low(kept, grad):
    return (low(grad),)
low.defvjp(low_keep, low_pass)
low_back.defvjp(back_keep, back_low)

def matmul(left, right):
    return jnp.dot(left, right, precision=lax.Precision.HIGHEST)

def rms_scale(values, gain):
    return values * lax.rsqrt(lax.optimization_barrier(jnp.mean(values * values, axis=-1, keepdims=True)) + epsilon) * gain

def rotate(values, positions):
    half_dim = values.shape[-1] // 2
    frequency = rope_base ** (-2.0 * jnp.arange(half_dim, dtype=jnp.float32) / values.shape[-1])
    angles = positions[:, None] * frequency[None, :]
    cosine = jnp.cos(angles)[:, None, :]
    sine_part = jnp.sin(angles)[:, None, :]
    lower_half = values[..., :half_dim]
    upper_half = values[..., half_dim:]
    return jnp.concatenate([lower_half * cosine - upper_half * sine_part, upper_half * cosine + lower_half * sine_part], axis=-1)

def conv_silu(raw, history, weight):
    padded = jnp.concatenate([history, raw], axis=0)
    row_count = raw.shape[0]
    conv_sum = sum((weight[kernel_step] * padded[kernel_step:kernel_step + row_count] for kernel_step in range(weight.shape[0])))
    return jax.nn.silu(conv_sum)

def ssd_block(state, x_heads, entry_map, read_map, step_size, decay_rate):
    row_count = step_size.shape[0]
    log_decay = jnp.cumsum(step_size * decay_rate, axis=0)
    causal = jnp.arange(row_count)[:, None] >= jnp.arange(row_count)[None, :]
    gap_log = log_decay.T[:, :, None] - log_decay.T[:, None, :]
    decay_mask = jnp.where(causal, jnp.exp(jnp.where(causal, gap_log, 0.0)), 0.0)
    scores = matmul(read_map, entry_map.T)
    weighted = x_heads * step_size[:, :, None]
    inner_part = jnp.einsum('hts,shp->thp', decay_mask * scores, weighted, precision=lax.Precision.HIGHEST)
    carried = jnp.einsum('tn,hpn->thp', read_map, state, precision=lax.Precision.HIGHEST) * jnp.exp(log_decay)[:, :, None]
    tail_weight = jnp.exp(log_decay[-1][None, :] - log_decay) * step_size
    local_state = jnp.einsum('sh,shp,sn->hpn', tail_weight, x_heads, entry_map, precision=lax.Precision.HIGHEST)
    new_state = jnp.exp(log_decay[-1])[:, None, None] * state + local_state
    return (new_state, inner_part + carried)

def attend(queries, keys, values):
    group_size = HQ // KV
    keys_wide = jnp.repeat(keys, group_size, axis=1)
    values_wide = jnp.repeat(values, group_size, axis=1)
    block_rows = min(512, LEN)
    key_pos = jnp.arange(LEN)

    def one_block(pieces):
        query_block, block_start = pieces
        scores = low_back(jnp.einsum('thd,shd->hts', query_block, keys_wide, precision=lax.Precision.HIGHEST) * HD ** (-0.5))
        query_pos = block_start + jnp.arange(block_rows)
        allowed = key_pos[None, :] <= query_pos[:, None]
        scores = jnp.where(allowed[None], scores, -1e+30)
        log_total = jax.nn.logsumexp(scores, axis=-1, keepdims=True)
        probs = low(jnp.exp(scores - log_total))
        return jnp.einsum('hts,shd->thd', probs, values_wide, precision=lax.Precision.HIGHEST)
    starts = jnp.arange(LEN // block_rows) * block_rows
    out_blocks = lax.map(jax.checkpoint(one_block), (queries.reshape(LEN // block_rows, block_rows, HQ, HD), starts))
    return out_blocks.reshape(LEN, HQ, HD)

def layer(params, row_in, decay_rate):
    norm_gain, mamba_in, mamba_bc, mamba_dt, dt_bias, conv_x, conv_bc, skip_d, ssm_gain, mamba_out, attn_q, attn_kv, attn_out, mlp_gain, mlp_gate_up, mlp_down = params
    positions = jnp.arange(LEN).astype(jnp.float32)
    normed = low(rms_scale(row_in, norm_gain))
    zx_proj = low_back(matmul(normed, mamba_in.reshape(D, 2 * DSSM))).reshape(LEN, 2, DSSM)
    bc_raw = matmul(normed, mamba_bc)
    dt_raw = low_back(matmul(normed, mamba_dt))
    x_conv = conv_silu(zx_proj[:, 1], jnp.zeros((CONV - 1, DSSM), jnp.float32), conv_x)
    bc_conv = conv_silu(bc_raw, jnp.zeros((CONV - 1, 2 * STATE), jnp.float32), conv_bc)
    step_size = jax.nn.softplus(dt_raw + dt_bias)
    x_heads = x_conv.reshape(LEN, HM, HD)
    blocks = LEN // TOK_DEV

    def scan_block(state, pieces):
        x_piece, entry_piece, read_piece, step_piece = pieces
        return ssd_block(state, x_piece, entry_piece, read_piece, step_piece, decay_rate)
    _, ssm_out = lax.scan(jax.checkpoint(scan_block), jnp.zeros((HM, HD, STATE), jnp.float32), (x_heads.reshape(blocks, TOK_DEV, HM, HD), bc_conv[:, :STATE].reshape(blocks, TOK_DEV, STATE), bc_conv[:, STATE:].reshape(blocks, TOK_DEV, STATE), step_size.reshape(blocks, TOK_DEV, HM)))
    ssm_out = ssm_out.reshape(LEN, HM, HD) + skip_d[None, :, None] * x_heads
    gated_y = ssm_out.reshape(LEN, DSSM) * jax.nn.silu(zx_proj[:, 0])
    ssm_scale = lax.rsqrt(lax.optimization_barrier(jnp.mean(gated_y * gated_y, axis=-1, keepdims=True)) + epsilon)
    mamba_part = low_back(matmul(low(gated_y * ssm_gain), mamba_out))
    queries = low(rotate(low_back(matmul(normed, attn_q)).reshape(LEN, HQ, HD), positions))
    kv_proj = low_back(matmul(normed, attn_kv.reshape(D, 2 * KV * HD))).reshape(LEN, 2, KV, HD)
    keys = low(rotate(kv_proj[:, 0], positions))
    values = low(kv_proj[:, 1])
    attn_vals = low_back(low(attend(queries, keys, values))).reshape(LEN, HQ * HD)
    mixed = low_back(matmul(attn_vals, attn_out) + ssm_scale * mamba_part)
    resid = row_in + mixed
    normed_two = low(rms_scale(resid, mlp_gain))
    gate_up = low_back(matmul(normed_two, mlp_gate_up.reshape(D, 2 * FF))).reshape(LEN, 2, FF)
    hidden = low(jax.nn.silu(gate_up[:, 0]) * gate_up[:, 1])
    return resid + matmul(hidden, mlp_down)

def reference(hidden_in, norm_gain, mamba_in, mamba_bc, mamba_dt, dt_bias, decay_seed, conv_x, conv_bc, skip_d, ssm_gain, mamba_out, attn_q, attn_kv, attn_out, mlp_gain, mlp_gate_up, mlp_down, cotangent):
    params = tuple((item.astype(jnp.float32) for item in (norm_gain, mamba_in, mamba_bc, mamba_dt, dt_bias, conv_x, conv_bc, skip_d, ssm_gain, mamba_out, attn_q, attn_kv, attn_out, mlp_gain, mlp_gate_up, mlp_down)))
    decay_rate = -jnp.exp(0.5 * decay_seed.astype(jnp.float32)) / LEN

    def per_sequence(totals, pieces):
        seq_in, seq_grad = pieces

        def apply_layer(weights, rows):
            return layer(weights, rows, decay_rate)
        result, pull = jax.vjp(apply_layer, params, seq_in.astype(jnp.float32))
        weight_grads, input_grad = pull(seq_grad.astype(jnp.float32))
        totals = jax.tree.map(jnp.add, totals, weight_grads)
        return (totals, (result.astype(jnp.bfloat16), input_grad.astype(jnp.bfloat16)))
    start_totals = jax.tree.map(jnp.zeros_like, params)
    totals, (block_out, grad_input) = lax.scan(per_sequence, start_totals, (hidden_in, cotangent))
    return (block_out, grad_input, totals[0], totals[1], totals[2], totals[3], totals[4], totals[5], totals[6], totals[7], totals[8], totals[9], totals[10], totals[11], totals[12], totals[13], totals[14], totals[15])
```

```python
from functools import partial

import jax
import jax.numpy as jnp
from jax import lax
from jax.sharding import PartitionSpec as P

D = 1024
HD = 64
STATE = 128
CONV = 4
DSSM = 1536


epsilon = 1e-05
rope_base = 100000000000.0


def passed_along(block, axis, distance):
    devices = range(lax.axis_size(axis))
    route = [(i - distance, i) for i in devices if i - distance in devices]
    return lax.ppermute(block, axis, route)


def swapped(block, axis, bit):
    return lax.ppermute(block, axis, [(i, i ^ bit) for i in range(lax.axis_size(axis))])


def bits_of(axis):
    return [1 << k for k in range(lax.axis_size(axis).bit_length() - 1)]


def pair_sum(block):
    return block + swapped(block, "tensor", 1).astype(block.dtype)


def near_first(values):
    count = lax.axis_size("shard")
    own = lax.axis_index("shard")
    width = values.shape[-1] // count
    return jnp.concatenate(
        [
            lax.dynamic_slice_in_dim(values, (own ^ j) * width, width, axis=values.ndim - 1)
            for j in range(count)
        ],
        axis=-1,
    )


def gathered_rows(block):
    bits = bits_of("shard")
    half = block.shape[0] // 2
    halves = []
    for part, order in ((block[:half], bits), (block[half:], bits[::-1])):
        pieces = {0: part}
        for bit in order:
            pieces.update({j ^ bit: swapped(p, "shard", bit) for j, p in list(pieces.items())})
        halves.append(pieces)
    return jnp.concatenate(
        [pieces[j] for j in range(lax.axis_size("shard")) for pieces in halves], axis=0
    )


def reduced_rows(left, right):
    count = lax.axis_size("shard")
    width = left.shape[1] // count
    columns = right.shape[1]
    cut = columns // 256 * 128
    bits = bits_of("shard")
    outs = []
    for part, order in ((right[:, :cut], bits), (right[:, cut:], bits[::-1])):
        pieces = {
            j: jnp.einsum(
                "td,tc->dc",
                left[:, j * width : (j + 1) * width],
                part,
                preferred_element_type=jnp.float32,
            )
            for j in range(count)
        }
        for bit in order:
            sent = {j: pieces.pop(j) for j in list(pieces) if j & bit}
            for j, piece in sent.items():
                pieces[j ^ bit] = pieces[j ^ bit] + swapped(
                    piece.astype(jnp.bfloat16), "shard", bit
                ).astype(jnp.float32)
        total = pieces[0]
        place = lax.axis_index("context")
        for bit in bits_of("context")[::-1]:
            rows = total.shape[0] // 2
            upper = (place // bit) % 2
            sent = lax.dynamic_slice_in_dim(total, (1 - upper) * rows, rows, axis=0)
            kept = lax.dynamic_slice_in_dim(total, upper * rows, rows, axis=0)
            total = kept + swapped(sent.astype(jnp.bfloat16), "context", bit).astype(jnp.float32)
        outs.append(total)
    return jnp.concatenate(outs, axis=1)


def summed_everywhere(block):
    for axis in ("shard", "context"):
        for bit in bits_of(axis):
            block = block + swapped(block, axis, bit)
    return block


def packed_state(decay, state):
    high = decay.astype(jnp.bfloat16)
    low = (decay - high.astype(jnp.float32)).astype(jnp.bfloat16)
    head = jnp.pad(jnp.stack([high, low]), ((0, 14), (0, STATE - decay.shape[0])))
    return jnp.concatenate([head, state.reshape(-1, STATE).astype(jnp.bfloat16)], axis=0)


def unpacked_state(packed, heads):
    decay = packed[0, :heads].astype(jnp.float32) + packed[1, :heads].astype(jnp.float32)
    return (decay, packed[16:].reshape(heads, HD, STATE).astype(jnp.float32))


def carried_state(decay, state, direction):
    heads = decay.shape[0]
    packed = packed_state(decay, state)
    weight = jnp.ones_like(decay)
    total = jnp.zeros_like(state)
    for distance in range(1, lax.axis_size("context")):
        far_decay, far_state = unpacked_state(
            passed_along(packed, "context", direction * distance), heads
        )
        total = total + weight[:, None, None] * far_state
        weight = weight * far_decay
    return total


def rms_scale(values, gain):
    return values * lax.rsqrt(jnp.mean(values * values, axis=-1, keepdims=True) + epsilon) * gain


def rotate(values, positions):
    half_dim = values.shape[-1] // 2
    frequency = rope_base ** (-2.0 * jnp.arange(half_dim, dtype=jnp.float32) / values.shape[-1])
    angles = positions[:, None] * frequency[None, :]
    cosine = jnp.cos(angles)[:, None, :]
    sine_part = jnp.sin(angles)[:, None, :]
    lower_half = values[..., :half_dim]
    upper_half = values[..., half_dim:]
    return jnp.concatenate(
        [
            lower_half * cosine - upper_half * sine_part,
            upper_half * cosine + lower_half * sine_part,
        ],
        axis=-1,
    )


def conv_silu(raw, history, weight):
    padded = jnp.concatenate([history, raw], axis=0)
    row_count = raw.shape[0]
    conv_sum = sum(
        (
            weight[kernel_step] * padded[kernel_step : kernel_step + row_count]
            for kernel_step in range(weight.shape[0])
        )
    )
    return jax.nn.silu(conv_sum)


def swiglu(gate_part, up_part):
    return jax.nn.silu(gate_part) * up_part


def section_one(raw_x, raw_bc, dt_raw, history, conv_x, conv_bc, dt_bias):
    x_width = raw_x.shape[1]
    x_conv = conv_silu(raw_x, history[:, :x_width], conv_x)
    bc_conv = conv_silu(raw_bc, history[:, x_width:], conv_bc)
    step_size = jax.nn.softplus(dt_raw + dt_bias)
    return (x_conv, bc_conv[:, :STATE], bc_conv[:, STATE:], step_size)


def section_two(x_conv, entry_map, read_map, step_size, skip_d, decay_rate):
    row_count = step_size.shape[0]
    head_count = step_size.shape[1]
    x_heads = x_conv.reshape(row_count, head_count, HD)
    log_decay = jnp.cumsum(step_size * decay_rate, axis=0)
    causal = jnp.arange(row_count)[:, None] >= jnp.arange(row_count)[None, :]
    gap_log = log_decay.T[:, :, None] - log_decay.T[:, None, :]
    decay_mask = jnp.where(causal, jnp.exp(jnp.where(causal, gap_log, 0.0)), 0.0)
    scores = jnp.dot(read_map, entry_map.T, precision=lax.Precision.HIGH)
    weighted = x_heads * step_size[:, :, None]
    inner_part = jnp.einsum(
        "hts,shp->thp", decay_mask * scores, weighted, precision=lax.Precision.HIGH
    )
    tail_weight = jnp.exp(log_decay[-1][None, :] - log_decay) * step_size
    local_state = jnp.einsum(
        "sh,shp,sn->hpn", tail_weight, x_heads, entry_map, precision=lax.Precision.HIGH
    )
    return (inner_part + skip_d[None, :, None] * x_heads, local_state, log_decay)


def section_three(y_local, state_in, read_map, log_decay, gate_z):
    carried = (
        jnp.einsum("tn,hpn->thp", read_map, state_in, precision=lax.Precision.HIGH)
        * jnp.exp(log_decay)[:, :, None]
    )
    ssm_out = (y_local + carried).reshape(y_local.shape[0], -1)
    return ssm_out * jax.nn.silu(gate_z)


def shards(
    hidden_in,
    norm_gain,
    mamba_in,
    mamba_bc,
    mamba_dt,
    dt_bias,
    decay_seed,
    conv_x,
    conv_bc,
    skip_d,
    ssm_gain,
    mamba_out,
    attn_q,
    attn_kv,
    attn_out,
    mlp_gain,
    mlp_gate_up,
    mlp_down,
    cotangent,
):
    rows_own = mamba_in.shape[0]
    x_width = mamba_in.shape[2]
    heads = mamba_dt.shape[1]
    dt_width = -(-heads // 128) * 128
    q_width = attn_q.shape[1]
    kv_width = attn_kv.shape[2]
    ff_local = mlp_gate_up.shape[2]
    scan_full = gathered_rows(
        jnp.concatenate(
            [mamba_in[:, 1], mamba_bc, jnp.pad(mamba_dt, ((0, 0), (0, dt_width - heads)))], axis=1
        )
    )
    side_full = gathered_rows(
        jnp.concatenate([mamba_in[:, 0], attn_q, attn_kv.reshape(rows_own, 2 * kv_width)], axis=1)
    )
    mix_full = gathered_rows(jnp.concatenate([mamba_out.T, attn_out.T], axis=1))
    mlp_full = gathered_rows(
        jnp.concatenate([mlp_gate_up.reshape(rows_own, 2 * ff_local), mlp_down.T], axis=1)
    )
    gu_full = mlp_full[:, : 2 * ff_local]
    down_full = mlp_full[:, 2 * ff_local :]
    mout_full = mix_full[:, :x_width]
    attn_full = mix_full[:, x_width:]
    norm_gain = near_first(norm_gain)
    mlp_gain = near_first(mlp_gain)
    row_in = near_first(hidden_in[0]).astype(jnp.float32)
    out_grad = near_first(cotangent[0])
    tok_rows = row_in.shape[0]
    seq_len = tok_rows * lax.axis_size("context")
    positions_int = lax.axis_index("context") * tok_rows + jnp.arange(tok_rows, dtype=jnp.int32)
    positions = positions_int.astype(jnp.float32)
    score_scale = HD ** (-0.5)
    normed_f, pull_norm_one = jax.vjp(rms_scale, row_in, norm_gain)
    normed = normed_f.astype(jnp.bfloat16)
    scan_proj = jnp.dot(normed, scan_full, preferred_element_type=jnp.float32)
    raw_x = scan_proj[:, :x_width]
    bc_raw = scan_proj[:, x_width : x_width + 2 * STATE]
    dt_raw = scan_proj[:, x_width + 2 * STATE : x_width + 2 * STATE + heads]
    side_proj = jnp.dot(normed, side_full, preferred_element_type=jnp.float32)
    gate_z = side_proj[:, :x_width]
    history = passed_along(
        scan_proj[tok_rows - (CONV - 1) :, : x_width + 2 * STATE], "context", 1
    )
    decay_rate = -jnp.exp(0.5 * decay_seed.astype(jnp.float32)) / seq_len
    (x_conv, entry_map, read_map, step_size), pull_one = jax.vjp(
        section_one, raw_x, bc_raw, dt_raw, history, conv_x, conv_bc, dt_bias
    )
    (y_local, state_local, log_decay), pull_two = jax.vjp(
        partial(section_two, decay_rate=decay_rate), x_conv, entry_map, read_map, step_size, skip_d
    )
    block_decay = jnp.exp(log_decay[-1])
    state_in = carried_state(block_decay, state_local, 1)
    gated_y, pull_three = jax.vjp(
        section_three, y_local, state_in, read_map, log_decay, gate_z
    )
    gated_b = (gated_y * ssm_gain).astype(jnp.bfloat16)
    mamba_part = jnp.einsum("tc,dc->td", gated_b, mout_full, preferred_element_type=jnp.float32)
    square_part = jnp.sum(gated_y * gated_y, axis=-1)
    query_heads = q_width // HD
    kv_heads = kv_width // HD
    group_size = query_heads // kv_heads
    query_pre = side_proj[:, x_width : x_width + q_width].reshape(
        tok_rows, query_heads, HD
    )
    queries = (
        rotate(query_pre, positions)
        .astype(jnp.bfloat16)
        .reshape(tok_rows, kv_heads, group_size, HD)
    )
    kv_pre = side_proj[:, x_width + q_width :].reshape(tok_rows, 2, kv_heads, HD)
    keys_local = rotate(kv_pre[:, 0], positions).astype(jnp.bfloat16)
    values_local = kv_pre[:, 1].astype(jnp.bfloat16)
    kv_send = jnp.stack([keys_local, values_local], axis=1).reshape(tok_rows, 2 * kv_heads * HD)
    blocks = lax.axis_size("context")
    kv_every = jnp.concatenate(
        [kv_send] + [passed_along(kv_send, "context", k) for k in range(1, blocks)], axis=0
    ).reshape(seq_len, 2, kv_heads, HD)
    keys_all = kv_every[:, 0]
    values_all = kv_every[:, 1]
    key_index = jnp.arange(seq_len, dtype=jnp.int32)
    back = key_index // tok_rows
    key_positions = (lax.axis_index("context") - back) * tok_rows + key_index % tok_rows
    allowed = (key_positions >= 0)[None, :] & (key_positions[None, :] <= positions_int[:, None])
    raw_scores = (
        jnp.einsum("tkgd,skd->kgts", queries, keys_all, preferred_element_type=jnp.float32)
        * score_scale
    )
    scores = jnp.where(allowed[None, None], raw_scores, -1e30)
    log_total = jax.nn.logsumexp(scores, axis=-1, keepdims=True)
    probs = jnp.exp(scores - log_total)
    probs_b = probs.astype(jnp.bfloat16)
    attn_vals = jnp.einsum(
        "kgts,skd->tkgd", probs_b, values_all, preferred_element_type=jnp.float32
    )
    attn_vals = attn_vals.astype(jnp.bfloat16).reshape(tok_rows, query_heads * HD)
    attn_part = jnp.einsum("th,dh->td", attn_vals, attn_full, preferred_element_type=jnp.float32)
    attn_sum = pair_sum(attn_part)
    mamba_sum = pair_sum(mamba_part)
    square_sum = pair_sum(square_part)
    ssm_scale = lax.rsqrt(square_sum / DSSM + epsilon)[:, None]
    resid = row_in + (attn_sum + ssm_scale * mamba_sum)
    normed_two_f, pull_norm_two = jax.vjp(rms_scale, resid, mlp_gain)
    normed_two = normed_two_f.astype(jnp.bfloat16)
    gate_up = jnp.dot(normed_two, gu_full, preferred_element_type=jnp.float32)
    hidden_f, pull_gate = jax.vjp(swiglu, gate_up[:, :ff_local], gate_up[:, ff_local:])
    hidden = hidden_f.astype(jnp.bfloat16)
    down_part = jnp.einsum("tf,df->td", hidden, down_full, preferred_element_type=jnp.float32)
    hidden_grad = jnp.dot(out_grad, down_full, preferred_element_type=jnp.float32)
    gate_grad, up_grad = pull_gate(hidden_grad)
    gate_up_grad = jnp.concatenate([gate_grad, up_grad], axis=1).astype(jnp.bfloat16)
    grad_down = reduced_rows(out_grad, hidden)
    grad_gate_up = reduced_rows(normed_two, gate_up_grad)
    normed_two_part = jnp.einsum(
        "tf,df->td", gate_up_grad, gu_full, preferred_element_type=jnp.float32
    )
    normed_two_grad = pair_sum(normed_two_part)
    resid_norm_grad, grad_mlp_gain = pull_norm_two(normed_two_grad)
    resid_grad = out_grad.astype(jnp.float32) + resid_norm_grad
    mixed_grad = resid_grad.astype(jnp.bfloat16)
    grad_attn_o = reduced_rows(mixed_grad, attn_vals)
    vals_grad = jnp.dot(mixed_grad, attn_full, preferred_element_type=jnp.float32)
    vals_grad = vals_grad.astype(jnp.bfloat16).reshape(tok_rows, kv_heads, group_size, HD)
    probs_grad = jnp.einsum(
        "tkgd,skd->kgts", vals_grad, values_all, preferred_element_type=jnp.float32
    )
    score_grad = (
        probs * (probs_grad - jnp.sum(probs * probs_grad, axis=-1, keepdims=True))
    ).astype(jnp.bfloat16)
    query_grad = (
        jnp.einsum("kgts,skd->tkgd", score_grad, keys_all, preferred_element_type=jnp.float32)
        * score_scale
    )
    key_grad_all = (
        jnp.einsum("kgts,tkgd->skd", score_grad, queries, preferred_element_type=jnp.float32)
        * score_scale
    )
    value_grad_all = jnp.einsum(
        "kgts,tkgd->skd", probs_b, vals_grad, preferred_element_type=jnp.float32
    )
    kv_grad_send = jnp.stack([key_grad_all, value_grad_all], axis=1).reshape(
        blocks, tok_rows, 2 * kv_heads * HD
    )
    kv_grad = kv_grad_send[0]
    for k in range(1, blocks):
        kv_grad = kv_grad + passed_along(
            kv_grad_send[k].astype(jnp.bfloat16), "context", -k
        ).astype(jnp.float32)
    kv_grad = kv_grad.reshape(tok_rows, 2, kv_heads, HD)
    query_pre_grad = rotate(query_grad.reshape(tok_rows, query_heads, HD), -positions)
    query_pre_grad = query_pre_grad.reshape(tok_rows, query_heads * HD).astype(jnp.bfloat16)
    key_pre_grad = rotate(kv_grad[:, 0], -positions)
    kv_pre_grad = (
        jnp.stack([key_pre_grad, kv_grad[:, 1]], axis=1)
        .reshape(tok_rows, 2 * kv_heads * HD)
        .astype(jnp.bfloat16)
    )
    mixed_f = mixed_grad.astype(jnp.float32)
    scale_grad = jnp.sum(mixed_f * mamba_sum, axis=-1, keepdims=True)
    mamba_grad = (ssm_scale * mixed_f).astype(jnp.bfloat16)
    grad_mout = reduced_rows(mamba_grad, gated_b)
    gated_grad = jnp.dot(mamba_grad, mout_full, preferred_element_type=jnp.float32)
    grad_ssm_gain = jnp.sum(gated_grad * gated_y, axis=0)
    y_grad = gated_grad * ssm_gain - scale_grad * ssm_scale * ssm_scale * ssm_scale * gated_y / DSSM
    y_local_grad, state_in_grad, read_grad_three, log_grad_three, gate_z_grad = pull_three(y_grad)
    state_out_grad = carried_state(block_decay, state_in_grad, -1)
    decay_grad = block_decay * jnp.sum(state_out_grad * state_in, axis=(1, 2))
    log_grad = log_grad_three.at[-1].add(decay_grad)
    x_conv_grad, entry_grad, read_grad_two, step_grad, grad_skip = pull_two(
        (y_local_grad, state_out_grad, log_grad)
    )
    raw_x_grad, bc_raw_grad, dt_raw_grad, history_grad, grad_conv_x, conv_bc_part, grad_dt_bias = (
        pull_one((x_conv_grad, entry_grad, read_grad_two + read_grad_three, step_grad))
    )
    tail_grad = passed_along(history_grad, "context", -1)
    raw_grad = (
        jnp.concatenate([raw_x_grad, bc_raw_grad], axis=1)
        .at[tok_rows - (CONV - 1) :]
        .add(tail_grad)
    )
    side_grad = jnp.concatenate(
        [gate_z_grad.astype(jnp.bfloat16), query_pre_grad, kv_pre_grad], axis=1
    )
    scan_grad = jnp.concatenate(
        [raw_grad, jnp.pad(dt_raw_grad, ((0, 0), (0, dt_width - heads)))], axis=1
    ).astype(jnp.bfloat16)
    side_total = reduced_rows(normed, side_grad)
    scan_total = reduced_rows(normed, scan_grad)
    normed_grad = jnp.einsum("tc,dc->td", side_grad, side_full, preferred_element_type=jnp.float32)
    normed_grad = normed_grad + jnp.einsum(
        "tc,dc->td", scan_grad, scan_full, preferred_element_type=jnp.float32
    )
    normed_sum = pair_sum(normed_grad)
    grad_bc = pair_sum(scan_total[:, x_width : x_width + 2 * STATE])
    down_sum = pair_sum(down_part)
    block_out = (resid + down_sum).astype(jnp.bfloat16)
    input_norm_grad, grad_norm_gain = pull_norm_one(normed_sum)
    grad_input = (resid_grad + input_norm_grad).astype(jnp.bfloat16)
    small = (
        near_first(grad_norm_gain),
        near_first(grad_mlp_gain),
        grad_ssm_gain,
        grad_conv_x,
        pair_sum(conv_bc_part),
        grad_dt_bias,
        grad_skip,
    )
    flat = jnp.concatenate([item.reshape(-1) for item in small])
    flat = jnp.pad(flat, (0, -flat.shape[0] % 1024)).reshape(-1, 128)
    flat = summed_everywhere(flat).reshape(-1)
    totals = []
    start = 0
    for item in small:
        totals.append(flat[start : start + item.size].reshape(item.shape))
        start += item.size
    small_norm, small_mlp, small_ssm, small_conv_x, small_conv_bc, small_dt_bias, small_skip = (
        totals
    )
    grad_in = jnp.stack([side_total[:, :x_width], scan_total[:, :x_width]], axis=1)
    return (
        near_first(block_out)[None],
        near_first(grad_input)[None],
        small_norm,
        grad_in,
        grad_bc,
        scan_total[:, x_width + 2 * STATE : x_width + 2 * STATE + heads],
        small_dt_bias,
        small_conv_x,
        small_conv_bc,
        small_skip,
        small_ssm,
        grad_mout.T,
        side_total[:, x_width : x_width + q_width],
        side_total[:, x_width + q_width :].reshape(-1, 2, kv_width),
        grad_attn_o.T,
        small_mlp,
        grad_gate_up.reshape(-1, 2, ff_local),
        grad_down.T,
    )


def solution(mesh):
    in_specs = (
        P("shard", "context", None),
        P(),
        P("shard", None, "tensor"),
        P("shard", None),
        P("shard", "tensor"),
        P("tensor"),
        P("tensor"),
        P(None, "tensor"),
        P(),
        P("tensor"),
        P("tensor"),
        P("tensor", "shard"),
        P("shard", "tensor"),
        P("shard", None, "tensor"),
        P("tensor", "shard"),
        P(),
        P("shard", None, "tensor"),
        P("tensor", "shard"),
        P("shard", "context", None),
    )
    out_specs = (
        P("shard", "context", None),
        P("shard", "context", None),
        P(),
        P(("shard", "context"), None, "tensor"),
        P(("shard", "context"), None),
        P(("shard", "context"), "tensor"),
        P("tensor"),
        P(None, "tensor"),
        P(),
        P("tensor"),
        P("tensor"),
        P("tensor", ("shard", "context")),
        P(("shard", "context"), "tensor"),
        P(("shard", "context"), None, "tensor"),
        P("tensor", ("shard", "context")),
        P(),
        P(("shard", "context"), None, "tensor"),
        P("tensor", ("shard", "context")),
    )
    return jax.shard_map(shards, mesh=mesh, in_specs=in_specs, out_specs=out_specs, check_vma=False)
```

```python
from functools import partial

import jax
import jax.numpy as jnp
from jax import lax
from jax.sharding import PartitionSpec as P

D = 1024
HD = 64
STATE = 128
CONV = 4
DSSM = 1536


epsilon = 1e-05
rope_base = 100000000000.0


def passed_along(block, axis, distance):
    devices = range(lax.axis_size(axis))
    route = [(i - distance, i) for i in devices if i - distance in devices]
    return lax.ppermute(block, axis, route)


def swapped(block, axis, bit):
    return lax.ppermute(block, axis, [(i, i ^ bit) for i in range(lax.axis_size(axis))])


def bits_of(axis):
    return [1 << k for k in range(lax.axis_size(axis).bit_length() - 1)]


def pair_sum(block):
    return block + swapped(block, "tensor", 1)


def short_pair_sum(block):
    sent = block.astype(jnp.bfloat16)
    return sent.astype(jnp.float32) + swapped(sent, "tensor", 1).astype(jnp.float32)


def near_first(values):
    count = lax.axis_size("shard")
    own = lax.axis_index("shard")
    width = values.shape[-1] // count
    return jnp.concatenate(
        [
            lax.dynamic_slice_in_dim(values, (own ^ j) * width, width, axis=values.ndim - 1)
            for j in range(count)
        ],
        axis=-1,
    )


def gathered_rows(block):
    bits = bits_of("shard")
    half = block.shape[0] // 2
    halves = []
    for part, order in ((block[:half], bits), (block[half:], bits[::-1])):
        pieces = {0: part}
        for bit in order:
            pieces.update({j ^ bit: swapped(p, "shard", bit) for j, p in list(pieces.items())})
        halves.append(pieces)
    return jnp.concatenate(
        [pieces[j] for j in range(lax.axis_size("shard")) for pieces in halves], axis=0
    )


def element(values):
    return lax.slice(values, (0,) * values.ndim, (1,) * values.ndim).reshape(()).astype(jnp.float32)


def after(values, token):
    return values if token is None else values + (0.0 * token).astype(values.dtype)


def reduced_rows(products, order, tokens=()):
    count = lax.axis_size("shard")
    waits = iter(tokens)
    pieces = {}
    for j in range(count):
        parts = []
        for left, right in products:
            width = left.shape[1] // count
            parts.append(
                jnp.einsum(
                    "td,tc->dc",
                    left[:, j * width : (j + 1) * width],
                    right,
                    preferred_element_type=jnp.float32,
                )
            )
        pieces[j] = parts
    sent_first = {j: [p.astype(jnp.bfloat16) for p in parts] for j, parts in pieces.items()}
    pieces = {
        j: jnp.concatenate(sent_first[j] if j & order[0] else parts, axis=1)
        for j, parts in pieces.items()
    }
    for bit in order:
        arrived = {
            j: swapped(pieces.pop(j).astype(jnp.bfloat16), "shard", bit)
            for j in list(pieces)
            if j & bit
        }
        token = next(waits, None)
        for j, piece in arrived.items():
            pieces[j ^ bit] = after(pieces[j ^ bit], token) + piece.astype(jnp.float32)
    total = pieces[0]
    place = lax.axis_index("context")
    for bit in bits_of("context")[::-1]:
        rows = total.shape[0] // 2
        upper = (place // bit) % 2
        sent = lax.dynamic_slice_in_dim(total, (1 - upper) * rows, rows, axis=0)
        kept = lax.dynamic_slice_in_dim(total, upper * rows, rows, axis=0)
        piece = swapped(sent.astype(jnp.bfloat16), "context", bit)
        total = after(kept, next(waits, None)) + piece.astype(jnp.float32)
    return total


def summed_everywhere(block):
    for axis in ("shard", "context"):
        for bit in bits_of(axis):
            block = block + swapped(block, axis, bit)
    return block


def packed_state(decay, state):
    high = decay.astype(jnp.bfloat16)
    low = (decay - high.astype(jnp.float32)).astype(jnp.bfloat16)
    head = jnp.pad(jnp.stack([high, low]), ((0, 14), (0, STATE - decay.shape[0])))
    return jnp.concatenate([head, state.reshape(-1, STATE).astype(jnp.bfloat16)], axis=0)


def unpacked_state(packed, heads):
    decay = packed[0, :heads].astype(jnp.float32) + packed[1, :heads].astype(jnp.float32)
    return (decay, packed[16:].reshape(heads, HD, STATE).astype(jnp.float32))


def carried_state(decay, state, direction):
    heads = decay.shape[0]
    packed = packed_state(decay, state)
    weight = jnp.ones_like(decay)
    total = jnp.zeros_like(state)
    for distance in range(1, lax.axis_size("context")):
        far_decay, far_state = unpacked_state(
            passed_along(packed, "context", direction * distance), heads
        )
        total = total + weight[:, None, None] * far_state
        weight = weight * far_decay
    return total


def rms_scale(values, gain):
    return values * lax.rsqrt(jnp.mean(values * values, axis=-1, keepdims=True) + epsilon) * gain


def rotate(values, positions):
    half_dim = values.shape[-1] // 2
    frequency = rope_base ** (-2.0 * jnp.arange(half_dim, dtype=jnp.float32) / values.shape[-1])
    angles = positions[:, None] * frequency[None, :]
    cosine = jnp.cos(angles)[:, None, :]
    sine_part = jnp.sin(angles)[:, None, :]
    lower_half = values[..., :half_dim]
    upper_half = values[..., half_dim:]
    return jnp.concatenate(
        [
            lower_half * cosine - upper_half * sine_part,
            upper_half * cosine + lower_half * sine_part,
        ],
        axis=-1,
    )


def conv_silu(raw, history, weight):
    padded = jnp.concatenate([history, raw], axis=0)
    row_count = raw.shape[0]
    conv_sum = sum(
        (
            weight[kernel_step] * padded[kernel_step : kernel_step + row_count]
            for kernel_step in range(weight.shape[0])
        )
    )
    return jax.nn.silu(conv_sum)


def swiglu(gate_part, up_part):
    return jax.nn.silu(gate_part) * up_part


def section_one(raw_x, raw_bc, dt_raw, history, conv_x, conv_bc, dt_bias):
    x_width = raw_x.shape[1]
    x_conv = conv_silu(raw_x, history[:, :x_width], conv_x)
    bc_conv = conv_silu(raw_bc, history[:, x_width:], conv_bc)
    step_size = jax.nn.softplus(dt_raw + dt_bias)
    return (x_conv, bc_conv[:, :STATE], bc_conv[:, STATE:], step_size)


def section_two(x_conv, entry_map, read_map, step_size, skip_d, decay_rate):
    row_count = step_size.shape[0]
    head_count = step_size.shape[1]
    x_heads = x_conv.reshape(row_count, head_count, HD)
    log_decay = jnp.cumsum(step_size * decay_rate, axis=0)
    causal = jnp.arange(row_count)[:, None] >= jnp.arange(row_count)[None, :]
    gap_log = log_decay.T[:, :, None] - log_decay.T[:, None, :]
    decay_mask = jnp.where(causal, jnp.exp(jnp.where(causal, gap_log, 0.0)), 0.0)
    scores = jnp.dot(read_map, entry_map.T, precision=lax.Precision.HIGH)
    weighted = x_heads * step_size[:, :, None]
    inner_part = jnp.einsum(
        "hts,shp->thp", decay_mask * scores, weighted, precision=lax.Precision.HIGH
    )
    tail_weight = jnp.exp(log_decay[-1][None, :] - log_decay) * step_size
    local_state = jnp.einsum(
        "sh,shp,sn->hpn", tail_weight, x_heads, entry_map, precision=lax.Precision.HIGH
    )
    return (inner_part + skip_d[None, :, None] * x_heads, local_state, log_decay)


def section_three(y_local, state_in, read_map, log_decay, gate_z):
    carried = (
        jnp.einsum("tn,hpn->thp", read_map, state_in, precision=lax.Precision.HIGH)
        * jnp.exp(log_decay)[:, :, None]
    )
    ssm_out = (y_local + carried).reshape(y_local.shape[0], -1)
    return ssm_out * jax.nn.silu(gate_z)


def shards(
    hidden_in,
    norm_gain,
    mamba_in,
    mamba_bc,
    mamba_dt,
    dt_bias,
    decay_seed,
    conv_x,
    conv_bc,
    skip_d,
    ssm_gain,
    mamba_out,
    attn_q,
    attn_kv,
    attn_out,
    mlp_gain,
    mlp_gate_up,
    mlp_down,
    cotangent,
):
    rows_own = mamba_in.shape[0]
    x_width = mamba_in.shape[2]
    heads = mamba_dt.shape[1]
    dt_width = -(-heads // 128) * 128
    q_width = attn_q.shape[1]
    kv_width = attn_kv.shape[2]
    ff_local = mlp_gate_up.shape[2]
    scan_full = gathered_rows(
        jnp.concatenate(
            [mamba_in[:, 1], mamba_bc, jnp.pad(mamba_dt, ((0, 0), (0, dt_width - heads)))], axis=1
        )
    )
    side_full = gathered_rows(
        jnp.concatenate([mamba_in[:, 0], attn_q, attn_kv.reshape(rows_own, 2 * kv_width)], axis=1)
    )
    norm_gain = near_first(norm_gain)
    mlp_gain = near_first(mlp_gain)
    row_in = near_first(hidden_in[0]).astype(jnp.float32)
    out_grad = near_first(cotangent[0])
    tok_rows = row_in.shape[0]
    seq_len = tok_rows * lax.axis_size("context")
    positions_int = lax.axis_index("context") * tok_rows + jnp.arange(tok_rows, dtype=jnp.int32)
    positions = positions_int.astype(jnp.float32)
    score_scale = HD ** (-0.5)
    normed_f, pull_norm_one = jax.vjp(rms_scale, row_in, norm_gain)
    normed = normed_f.astype(jnp.bfloat16)
    scan_proj = jnp.dot(normed, scan_full, preferred_element_type=jnp.float32)
    raw_x = scan_proj[:, :x_width]
    bc_raw = scan_proj[:, x_width : x_width + 2 * STATE]
    dt_raw = scan_proj[:, x_width + 2 * STATE : x_width + 2 * STATE + heads]
    scan_token = element(scan_proj)
    mix_full = gathered_rows(
        after(jnp.concatenate([mamba_out.T, attn_out.T], axis=1), scan_token)
    )
    mlp_full = gathered_rows(
        after(
            jnp.concatenate(
                [mlp_gate_up.reshape(rows_own, 2 * ff_local), mlp_down.T], axis=1
            ),
            scan_token,
        )
    )
    gu_full = mlp_full[:, : 2 * ff_local]
    down_full = mlp_full[:, 2 * ff_local :]
    mout_full = mix_full[:, :x_width]
    attn_full = mix_full[:, x_width:]
    side_proj = jnp.dot(normed, side_full, preferred_element_type=jnp.float32)
    gate_z = side_proj[:, :x_width]
    history = passed_along(
        scan_proj[tok_rows - (CONV - 1) :, : x_width + 2 * STATE], "context", 1
    )
    decay_rate = -jnp.exp(0.5 * decay_seed.astype(jnp.float32)) / seq_len
    (x_conv, entry_map, read_map, step_size), pull_one = jax.vjp(
        section_one, raw_x, bc_raw, dt_raw, history, conv_x, conv_bc, dt_bias
    )
    (y_local, state_local, log_decay), pull_two = jax.vjp(
        partial(section_two, decay_rate=decay_rate), x_conv, entry_map, read_map, step_size, skip_d
    )
    block_decay = jnp.exp(log_decay[-1])
    state_in = carried_state(block_decay, state_local, 1)
    gated_y, pull_three = jax.vjp(
        section_three, y_local, state_in, read_map, log_decay, gate_z
    )
    gated_b = (gated_y * ssm_gain).astype(jnp.bfloat16)
    mamba_part = jnp.einsum("tc,dc->td", gated_b, mout_full, preferred_element_type=jnp.float32)
    square_part = jnp.sum(gated_y * gated_y, axis=-1)
    query_heads = q_width // HD
    kv_heads = kv_width // HD
    group_size = query_heads // kv_heads
    query_pre = side_proj[:, x_width : x_width + q_width].reshape(
        tok_rows, query_heads, HD
    )
    queries = (
        rotate(query_pre, positions)
        .astype(jnp.bfloat16)
        .reshape(tok_rows, kv_heads, group_size, HD)
    )
    kv_pre = side_proj[:, x_width + q_width :].reshape(tok_rows, 2, kv_heads, HD)
    keys_local = rotate(kv_pre[:, 0], positions).astype(jnp.bfloat16)
    values_local = kv_pre[:, 1].astype(jnp.bfloat16)
    kv_send = jnp.stack([keys_local, values_local], axis=1).reshape(tok_rows, 2 * kv_heads * HD)
    blocks = lax.axis_size("context")
    kv_every = jnp.concatenate(
        [kv_send] + [passed_along(kv_send, "context", k) for k in range(1, blocks)], axis=0
    ).reshape(seq_len, 2, kv_heads, HD)
    keys_all = kv_every[:, 0]
    values_all = kv_every[:, 1]
    key_index = jnp.arange(seq_len, dtype=jnp.int32)
    back = key_index // tok_rows
    key_positions = (lax.axis_index("context") - back) * tok_rows + key_index % tok_rows
    allowed = (key_positions >= 0)[None, :] & (key_positions[None, :] <= positions_int[:, None])
    raw_scores = (
        jnp.einsum("tkgd,skd->kgts", queries, keys_all, preferred_element_type=jnp.float32)
        * score_scale
    )
    scores = jnp.where(allowed[None, None], raw_scores, -1e30)
    log_total = jax.nn.logsumexp(scores, axis=-1, keepdims=True)
    probs = jnp.exp(scores - log_total)
    probs_b = probs.astype(jnp.bfloat16)
    attn_vals = jnp.einsum(
        "kgts,skd->tkgd", probs_b, values_all, preferred_element_type=jnp.float32
    )
    attn_vals = attn_vals.astype(jnp.bfloat16).reshape(tok_rows, query_heads * HD)
    attn_part = jnp.einsum("th,dh->td", attn_vals, attn_full, preferred_element_type=jnp.float32)
    attn_sum = pair_sum(attn_part)
    mamba_sum = pair_sum(mamba_part)
    square_sum = pair_sum(square_part)
    ssm_scale = lax.rsqrt(square_sum / DSSM + epsilon)[:, None]
    resid = row_in + (attn_sum + ssm_scale * mamba_sum)
    normed_two_f, pull_norm_two = jax.vjp(rms_scale, resid, mlp_gain)
    normed_two = normed_two_f.astype(jnp.bfloat16)
    gate_up = jnp.dot(normed_two, gu_full, preferred_element_type=jnp.float32)
    hidden_f, pull_gate = jax.vjp(swiglu, gate_up[:, :ff_local], gate_up[:, ff_local:])
    hidden = hidden_f.astype(jnp.bfloat16)
    down_part = jnp.einsum("tf,df->td", hidden, down_full, preferred_element_type=jnp.float32)
    hidden_grad = jnp.dot(out_grad, down_full, preferred_element_type=jnp.float32)
    gate_grad, up_grad = pull_gate(hidden_grad)
    gate_up_grad = jnp.concatenate([gate_grad, up_grad], axis=1).astype(jnp.bfloat16)
    normed_two_part = jnp.einsum(
        "tf,df->td", gate_up_grad, gu_full, preferred_element_type=jnp.float32
    )
    normed_two_grad = pair_sum(normed_two_part)
    resid_norm_grad, grad_mlp_gain = pull_norm_two(normed_two_grad)
    resid_grad = out_grad.astype(jnp.float32) + resid_norm_grad
    mixed_grad = resid_grad.astype(jnp.bfloat16)
    vals_grad = jnp.dot(mixed_grad, attn_full, preferred_element_type=jnp.float32)
    vals_grad = vals_grad.astype(jnp.bfloat16).reshape(tok_rows, kv_heads, group_size, HD)
    probs_grad = jnp.einsum(
        "tkgd,skd->kgts", vals_grad, values_all, preferred_element_type=jnp.float32
    )
    score_grad = (
        probs * (probs_grad - jnp.sum(probs * probs_grad, axis=-1, keepdims=True))
    ).astype(jnp.bfloat16)
    query_grad = (
        jnp.einsum("kgts,skd->tkgd", score_grad, keys_all, preferred_element_type=jnp.float32)
        * score_scale
    )
    key_grad_all = (
        jnp.einsum("kgts,tkgd->skd", score_grad, queries, preferred_element_type=jnp.float32)
        * score_scale
    )
    value_grad_all = jnp.einsum(
        "kgts,tkgd->skd", probs_b, vals_grad, preferred_element_type=jnp.float32
    )
    kv_grad_send = jnp.stack([key_grad_all, value_grad_all], axis=1).reshape(
        blocks, tok_rows, 2 * kv_heads * HD
    )
    kv_grad = kv_grad_send[0]
    for k in range(1, blocks):
        kv_grad = kv_grad + passed_along(
            kv_grad_send[k].astype(jnp.bfloat16), "context", -k
        ).astype(jnp.float32)
    kv_grad = kv_grad.reshape(tok_rows, 2, kv_heads, HD)
    query_pre_grad = rotate(query_grad.reshape(tok_rows, query_heads, HD), -positions)
    query_pre_grad = query_pre_grad.reshape(tok_rows, query_heads * HD).astype(jnp.bfloat16)
    key_pre_grad = rotate(kv_grad[:, 0], -positions)
    kv_pre_grad = (
        jnp.stack([key_pre_grad, kv_grad[:, 1]], axis=1)
        .reshape(tok_rows, 2 * kv_heads * HD)
        .astype(jnp.bfloat16)
    )
    mixed_f = mixed_grad.astype(jnp.float32)
    scale_grad = jnp.sum(mixed_f * mamba_sum, axis=-1, keepdims=True)
    mamba_grad = (ssm_scale * mixed_f).astype(jnp.bfloat16)
    gated_grad = jnp.dot(mamba_grad, mout_full, preferred_element_type=jnp.float32)
    grad_ssm_gain = jnp.sum(gated_grad * gated_y, axis=0)
    y_grad = gated_grad * ssm_gain - scale_grad * ssm_scale * ssm_scale * ssm_scale * gated_y / DSSM
    y_local_grad, state_in_grad, read_grad_three, log_grad_three, gate_z_grad = pull_three(y_grad)
    state_out_grad = carried_state(block_decay, state_in_grad, -1)
    decay_grad = block_decay * jnp.sum(state_out_grad * state_in, axis=(1, 2))
    log_grad = log_grad_three.at[-1].add(decay_grad)
    x_conv_grad, entry_grad, read_grad_two, step_grad, grad_skip = pull_two(
        (y_local_grad, state_out_grad, log_grad)
    )
    raw_x_grad, bc_raw_grad, dt_raw_grad, history_grad, grad_conv_x, conv_bc_part, grad_dt_bias = (
        pull_one((x_conv_grad, entry_grad, read_grad_two + read_grad_three, step_grad))
    )
    tail_grad = passed_along(history_grad, "context", -1)
    raw_grad = (
        jnp.concatenate([raw_x_grad, bc_raw_grad], axis=1)
        .at[tok_rows - (CONV - 1) :]
        .add(tail_grad)
    )
    side_grad = jnp.concatenate(
        [gate_z_grad.astype(jnp.bfloat16), query_pre_grad, kv_pre_grad], axis=1
    )
    scan_grad = jnp.concatenate(
        [raw_grad, jnp.pad(dt_raw_grad, ((0, 0), (0, dt_width - heads)))], axis=1
    ).astype(jnp.bfloat16)
    bits = bits_of("shard")
    tokens = (
        element(kv_grad_send) + element(state_in_grad),
        element(state_out_grad),
        element(x_conv_grad) + element(step_grad),
        element(raw_x_grad),
    )
    late_total = reduced_rows(
        [(normed_two, gate_up_grad[:, :ff_local]), (mixed_grad, attn_vals), (mamba_grad, gated_b)],
        bits,
        tokens,
    )
    down_total = reduced_rows(
        [(normed_two, gate_up_grad[:, ff_local:]), (out_grad, hidden)], bits[::-1], tokens
    )
    grad_gate_up = jnp.stack([late_total[:, :ff_local], down_total[:, :ff_local]], axis=1)
    grad_attn_o = late_total[:, ff_local : ff_local + q_width]
    grad_mout = late_total[:, ff_local + q_width :]
    grad_down = down_total[:, ff_local:]
    side_total = reduced_rows([(normed, side_grad)], bits)
    cut = scan_grad.shape[1] // 256 * 128
    scan_total = jnp.concatenate(
        [
            reduced_rows([(normed, scan_grad[:, :cut])], bits),
            reduced_rows([(normed, scan_grad[:, cut:])], bits[::-1]),
        ],
        axis=1,
    )
    normed_grad = jnp.einsum("tc,dc->td", side_grad, side_full, preferred_element_type=jnp.float32)
    normed_grad = normed_grad + jnp.einsum(
        "tc,dc->td", scan_grad, scan_full, preferred_element_type=jnp.float32
    )
    normed_sum = short_pair_sum(normed_grad)
    grad_bc = pair_sum(scan_total[:, x_width : x_width + 2 * STATE])
    down_sum = short_pair_sum(down_part)
    block_out = (resid + down_sum).astype(jnp.bfloat16)
    input_norm_grad, grad_norm_gain = pull_norm_one(normed_sum)
    grad_input = (resid_grad + input_norm_grad).astype(jnp.bfloat16)
    small = (
        near_first(grad_norm_gain),
        near_first(grad_mlp_gain),
        grad_ssm_gain,
        grad_conv_x,
        pair_sum(conv_bc_part),
        grad_dt_bias,
        grad_skip,
    )
    flat = jnp.concatenate([item.reshape(-1) for item in small])
    flat = jnp.pad(flat, (0, -flat.shape[0] % 1024)).reshape(-1, 128)
    flat = summed_everywhere(flat).reshape(-1)
    totals = []
    start = 0
    for item in small:
        totals.append(flat[start : start + item.size].reshape(item.shape))
        start += item.size
    small_norm, small_mlp, small_ssm, small_conv_x, small_conv_bc, small_dt_bias, small_skip = (
        totals
    )
    grad_in = jnp.stack([side_total[:, :x_width], scan_total[:, :x_width]], axis=1)
    return (
        near_first(block_out)[None],
        near_first(grad_input)[None],
        small_norm,
        grad_in,
        grad_bc,
        scan_total[:, x_width + 2 * STATE : x_width + 2 * STATE + heads],
        small_dt_bias,
        small_conv_x,
        small_conv_bc,
        small_skip,
        small_ssm,
        grad_mout.T,
        side_total[:, x_width : x_width + q_width],
        side_total[:, x_width + q_width :].reshape(-1, 2, kv_width),
        grad_attn_o.T,
        small_mlp,
        grad_gate_up,
        grad_down.T,
    )


def solution(mesh):
    in_specs = (
        P("shard", "context", None),
        P(),
        P("shard", None, "tensor"),
        P("shard", None),
        P("shard", "tensor"),
        P("tensor"),
        P("tensor"),
        P(None, "tensor"),
        P(),
        P("tensor"),
        P("tensor"),
        P("tensor", "shard"),
        P("shard", "tensor"),
        P("shard", None, "tensor"),
        P("tensor", "shard"),
        P(),
        P("shard", None, "tensor"),
        P("tensor", "shard"),
        P("shard", "context", None),
    )
    out_specs = (
        P("shard", "context", None),
        P("shard", "context", None),
        P(),
        P(("shard", "context"), None, "tensor"),
        P(("shard", "context"), None),
        P(("shard", "context"), "tensor"),
        P("tensor"),
        P(None, "tensor"),
        P(),
        P("tensor"),
        P("tensor"),
        P("tensor", ("shard", "context")),
        P(("shard", "context"), "tensor"),
        P(("shard", "context"), None, "tensor"),
        P("tensor", ("shard", "context")),
        P(),
        P(("shard", "context"), None, "tensor"),
        P("tensor", ("shard", "context")),
    )
    return jax.shard_map(shards, mesh=mesh, in_specs=in_specs, out_specs=out_specs, check_vma=False)
```
